32 devices in a mesh: tt: 4 (over y, x), sv: 8 (over z, core).
Axes of the slice: x: 2, y: 2, z: 4, core: 2. Of those that a mesh axis runs over, the one named last changes fastest.
Arguments:
- teacher_hidden: bfloat16 [64, 16384], P(None, 'sv'), may hold values from -620 to 620
- teacher_head: bfloat16 [16384, 65536], P('sv', 'tt'), may hold values from -0.046875 to 0.046875
- student_hidden: bfloat16 [64, 4096], P(('tt', 'sv')), may hold values from -42 to 42
- student_head: bfloat16 [4096, 65536], P(None, ('tt', 'sv')), may hold values from -1.5 to 1.5
- targets: int32 [64], replicated, may hold values from 0 to 65535
Outputs:
- loss: float32 [], replicated
- head_grad: bfloat16 [4096, 65536], P(None, ('tt', 'sv'))
- hidden_grad: float32 [64, 4096], P(('tt', 'sv'))
The draws below stay inside these ranges and needn't reach their ends.
All inputs are finite; a program needn't handle non-finite values.
Results may differ from the reference program's by a relative error of at most 0.0038.
Values may be sent and summed in bfloat16 or wider, within the bound.
A program may use at most 192 MiB of HBM per device.

```python
import math
import jax
import jax.numpy as jnp
from jax import lax

DT = 16384
DS = 4096
V = 65536
TOKENS = 64


def row_factors(key, rows, low, high, boost):
    key_scale, key_boost = jax.random.split(key)
    scale = jnp.exp(jax.random.uniform(key_scale, (rows, 1), jnp.float32, math.log(low), math.log(high)))
    picks = jax.random.randint(key_boost, (rows, 1), 0, 16)
    return scale * jnp.where(picks == 0, boost, 1.0)


def draw_teacher_hidden(key, part):
    key = jax.random.fold_in(key, 11)
    key_base, key_rows = jax.random.split(key)
    base = jnp.clip(jax.random.normal(key_base, (TOKENS, DT), jnp.float32), -6.0, 6.0)
    factors = row_factors(key_rows, TOKENS, 3.0, 30.0, 1.0)
    return (base * factors).astype(jnp.bfloat16)


def draw_student_hidden(key, part):
    key = jax.random.fold_in(key, 23)
    key_base, key_rows = jax.random.split(key)
    base = jnp.clip(jax.random.normal(key_base, (TOKENS, DS), jnp.float32), -6.0, 6.0)
    factors = row_factors(key_rows, TOKENS, 0.2, 2.0, 1.0)
    return (base * factors).astype(jnp.bfloat16)


def touch_ends(array, key, low, high):
    longest = array.shape.index(max(array.shape))
    spots = []
    for shift in (0, 1):
        where = [jax.random.randint(jax.random.fold_in(key, axis), (), 0, length) for axis, length in enumerate(array.shape)]
        where[longest] = (where[longest] + shift) % array.shape[longest]
        spots.append(tuple(where))
    return array.at[spots[0]].set(low).at[spots[1]].set(high)


def block_scale(stream_key, extent, pieces, smallest, high):
    loudness = 1.0
    for axis_at, parts in pieces:
        steps = jax.random.uniform(jax.random.fold_in(jax.random.fold_in(stream_key, 6), axis_at), (parts,), jnp.float32, smallest / len(pieces), high / len(pieces))
        loudness = loudness * jnp.repeat(jnp.exp(steps), extent[axis_at] // parts).reshape((-1,) + (1,) * (len(extent) - 1 - axis_at))
    return loudness


def scatter_about(own_key, shape, width, limit, cuts=(), dtype=jnp.bfloat16):
    result = width * jax.random.normal(own_key, shape, jnp.float32)
    if cuts:
        result = result * block_scale(own_key, shape, cuts, -0.22, 0.18)
    return jnp.clip(result, -limit, limit).astype(dtype)


def setup_inputs(seed: int = 0) -> dict:
    arg_keys = jax.random.split(jax.random.key(seed), 6)
    teacher_hidden = draw_teacher_hidden(jax.random.fold_in(arg_keys[5], 71), 0)
    teacher_head = scatter_about(arg_keys[1], (DT, V), DT ** -0.5, 0.046875, ((0, 8), (1, 4)))
    student_hidden = draw_student_hidden(jax.random.fold_in(arg_keys[5], 71), 0)
    student_head = scatter_about(arg_keys[3], (DS, V), 0.25, 1.5, ((1, 32),))
    targets = touch_ends(jax.random.randint(arg_keys[4], (TOKENS,), 0, V), jax.random.fold_in(arg_keys[4], 1), 0, V - 1).astype(jnp.int32)
    return {"teacher_hidden": teacher_hidden, "teacher_head": teacher_head, "student_hidden": student_hidden, "student_head": student_head, "targets": targets}


ce_weight = 0.5


def log_softmax_rows(logits):
    top = jnp.max(logits, axis=1, keepdims=True)
    return logits - (top + jnp.log(jnp.sum(jnp.exp(logits - top), axis=1, keepdims=True)))


def reference(teacher_hidden, teacher_head, student_hidden, student_head, targets):
    tokens = teacher_hidden.shape[0]
    logits_t = jnp.dot(teacher_hidden, teacher_head, preferred_element_type=jnp.float32)
    log_t = log_softmax_rows(logits_t)
    rounded = lax.optimization_barrier(jnp.exp(log_t).astype(jnp.bfloat16))
    probs = rounded.astype(jnp.float32)
    entropy = jnp.sum(probs * log_t)
    logits_s = jnp.dot(student_hidden, student_head, preferred_element_type=jnp.float32)
    top = jnp.max(logits_s, axis=1)
    norm_s = top + jnp.log(jnp.sum(jnp.exp(logits_s - top[:, None]), axis=1))
    columns = lax.broadcasted_iota(jnp.int32, (1, logits_s.shape[1]), 1)
    hit = (columns == targets.astype(jnp.int32)[:, None]).astype(jnp.float32)
    cross = jnp.sum(probs * logits_s, axis=1)
    mass = jnp.sum(probs, axis=1)
    picked = jnp.sum(hit * logits_s, axis=1)
    loss = (entropy - jnp.sum(cross - mass * norm_s) + ce_weight * jnp.sum(norm_s - picked)) / tokens
    probs_s = jnp.exp(logits_s - norm_s[:, None])
    grad_logits = ((mass + ce_weight)[:, None] * probs_s - probs - ce_weight * hit).astype(jnp.bfloat16)
    head_grad = jnp.dot(student_hidden.T, grad_logits, preferred_element_type=jnp.float32).astype(jnp.bfloat16)
    hidden_grad = jnp.dot(grad_logits, student_head.T, preferred_element_type=jnp.float32)
    return loss, head_grad, hidden_grad
```

```python
import functools

import jax
import jax.numpy as jnp
from jax import lax
from jax.experimental import pallas as pl
from jax.experimental.pallas import tpu as pltpu
from jax.sharding import PartitionSpec as P

MESH = pl.DeviceIdType.MESH
ce_weight = 0.5
depth = 6


def visit_order(nz):
    table = []
    for z in range(nz):
        right, left = list(range(nz - 1, z, -1)), list(range(z))
        first, second = (right, left) if len(right) >= len(left) else (left, right)
        order = []
        while first or second:
            if first:
                order.append(first.pop(0))
            if second:
                order.append(second.pop(0))
        table.append(order + [z])
    return table


def lookup(table, row, column):
    value = jnp.int32(0)
    for r, entries in enumerate(table):
        for c, entry in enumerate(entries):
            if entry:
                value = jnp.where((row == r) & (column == c), jnp.int32(entry), value)
    return value


def kernel(
    ntt, nv, nq,
    t_hidden, t_head, s_hidden, s_head, targets,
    loss_ref, hid_ref, grad_ref, hgrad_ref,
    t_buf, w_buf, mine, sib_out, sib_in, line_in, logits_t, logits_s,
    hid_all, hid_f, stat_all, hg_out, hg_in, hg_own, tt_out, tt_in, z_out, z_in, c_out, c_in,
    t_sem, w_sem, sib_send, sib_recv, line_send, line_recv,
    hid_send, hid_recv, stat_send, stat_recv, hg_send, hg_recv, tt_send, tt_recv, z_send, z_recv,
):
    nz = nv // 2
    tt, sv = lax.axis_index("tt"), lax.axis_index("sv")
    z, core = sv // 2, sv % 2
    tokens = t_hidden.shape[0]
    vd = s_head.shape[1]
    ds = s_head.shape[0]
    cw = vd // nq
    steps = nz * nq
    table = visit_order(nz)

    def other_z(k):
        return lax.rem(z + k, nz)

    def other_tt(k):
        return lax.rem(tt + k, ntt)

    def push(src, dst, send, recv, where):
        return pltpu.make_async_remote_copy(
            src_ref=src, dst_ref=dst, send_sem=send, recv_sem=recv, device_id=where, device_id_type=MESH
        )

    sibling = {"sv": z * 2 + (1 - core)}

    def piece(i):
        s, half = i // 2, i % 2
        dest = lookup(table, z, s // nq)
        who = jnp.where(half == 0, 1 - core, core)
        start = pl.multiple_of((dest * 2 + who) * vd + (s % nq) * cw, 128)
        slot = lax.rem(i, depth)
        return pltpu.make_async_copy(t_head.at[:, pl.ds(start, cw)], t_buf.at[slot], t_sem.at[slot])

    for i in range(min(depth, 2 * steps)):
        piece(jnp.int32(i)).start()
    student = pltpu.make_async_copy(s_head, w_buf, w_sem)

    barrier = pltpu.get_barrier_semaphore()
    pl.semaphore_signal(barrier, inc=1, device_id=sibling, device_id_type=MESH)
    for k in range(1, nz):
        pl.semaphore_signal(barrier, inc=1, device_id={"sv": other_z(k) * 2 + core}, device_id_type=MESH)
    for k in range(1, ntt):
        pl.semaphore_signal(barrier, inc=1, device_id={"tt": other_tt(k)}, device_id_type=MESH)
    pl.semaphore_wait(barrier, nz + ntt - 1)

    def gather_z(buf, send, recv):
        return [
            push(buf.at[core, tt, z], buf.at[core, tt, z], send.at[k], recv.at[z], {"sv": other_z(k) * 2 + core})
            for k in range(1, nz)
        ]

    def gather_z_wait(buf, send, recv):
        for k in range(1, nz):
            p = other_z(k)
            push(buf.at[core, tt, p], buf.at[core, tt, p], send.at[k], recv.at[p], {"sv": p * 2 + core}).wait_recv()

    def gather_tt(buf, send, recv):
        return [
            push(buf.at[core, tt], buf.at[core, tt], send.at[nz + k], recv.at[nz + tt], {"tt": other_tt(k)})
            for k in range(1, ntt)
        ]

    def gather_tt_wait(buf, send, recv):
        for k in range(1, ntt):
            p = other_tt(k)
            push(buf.at[core, p], buf.at[core, p], send.at[nz + k], recv.at[nz + p], {"tt": p}).wait_recv()

    def gather_core(buf, send, recv):
        return push(buf.at[core], buf.at[core], send.at[0], recv.at[nz + ntt], sibling)

    def gather_core_wait(buf, send, recv):
        push(buf.at[1 - core], buf.at[1 - core], send.at[0], recv.at[nz + ntt], sibling).wait_recv()

    def start_all(copies):
        for copy in copies:
            copy.start()

    def gather_sent(buf, send, recv):
        for copy in gather_z(buf, send, recv) + gather_tt(buf, send, recv) + [gather_core(buf, send, recv)]:
            copy.wait_send()

    hid_gather = (hid_all, hid_send, hid_recv)
    hid_all[core, tt, z] = s_hidden[...].astype(jnp.float32)
    start_all(gather_z(*hid_gather))

    def sib_copy(s):
        dest, q = lookup(table, z, s // nq), s % nq
        return push(sib_out.at[dest, q], sib_in.at[dest, q], sib_send.at[s], sib_recv.at[s], sibling)

    def line_copy(s):
        dest, q = lookup(table, z, s // nq), s % nq
        side = jnp.where(dest > z, 0, 1)
        onto = jnp.where(dest > z, z + 1, z - 1)
        return push(
            mine.at[dest, q], line_in.at[side, dest, q], line_send.at[s], line_recv.at[side, dest, q],
            {"sv": onto * 2 + core},
        )

    def line_arrived(side, dest, q):
        ref = line_in.at[side, dest, q]
        push(ref, ref, line_send.at[0], line_recv.at[side, dest, q], sibling).wait_recv()

    def pair(s):
        sib_copy(s).wait_recv()
        dest, q = lookup(table, z, s // nq), s % nq
        mine[dest, q] += sib_in[dest, q]

    def forward(s):
        dest, q = lookup(table, z, s // nq), s % nq
        side = jnp.where(dest > z, 0, 1)
        upstream = jnp.where(dest > z, z > 0, z < nz - 1)

        @pl.when(upstream)
        def _():
            line_arrived(side, dest, q)
            mine[dest, q] += line_in[side, dest, q]

        line_copy(s).start()

    outer = (nz - 1) * nq
    at_end = (z == 0) | (z == nz - 1)

    @pl.loop(0, steps)
    def _(s):
        dest, q = lookup(table, z, s // nq), s % nq
        for half, target in ((0, sib_out), (1, mine)):
            i = 2 * s + half
            piece(i).wait()
            target[dest, q] = jnp.dot(
                t_hidden[...], t_buf[lax.rem(i, depth)], preferred_element_type=jnp.float32
            )
            if half == 0:
                sib_copy(s).start()

            @pl.when(i + depth < 2 * steps)
            def _():
                piece(i + depth).start()

        @pl.when(s == max(0, steps - 4))
        def _():
            student.start()

        @pl.when(s >= 1)
        def _():
            pair(s - 1)

        late = jnp.where(at_end, s - 1, s - 2)

        @pl.when((late >= 0) & (late < outer))
        def _():
            forward(late)

        @pl.when(s == steps // 4)
        def _():
            gather_z_wait(*hid_gather)
            start_all(gather_tt(*hid_gather))

        @pl.when(s == steps // 2)
        def _():
            gather_tt_wait(*hid_gather)
            gather_core(*hid_gather).start()

    pair(jnp.int32(steps - 1))
    for late in range(max(0, steps - 2), outer):

        @pl.when(jnp.logical_not(at_end) | (late >= steps - 1))
        def _():
            forward(jnp.int32(late))

    gather_core_wait(*hid_gather)
    rows = s_hidden.shape[0]
    for a in range(ntt):
        for b in range(nz):
            for c in range(2):
                at = (a * nv + b * 2 + c) * rows
                hid_f[at : at + rows, :] = hid_all[c, a, b]
    hid_ref[...] = hid_f[...].astype(jnp.bfloat16)

    student.wait()

    @pl.loop(0, nq)
    def _(n):
        logits_s[n] = jnp.dot(
            hid_ref[...], w_buf[:, pl.ds(pl.multiple_of(n * cw, 128), cw)], preferred_element_type=jnp.float32
        )

    for q in range(nq):
        logits_t[q] = mine[z, q]
        for side, there in ((0, z > 0), (1, z < nz - 1)):

            @pl.when(there)
            def _():
                line_arrived(side, z, q)
                logits_t[q] += line_in[side, z, q]

    offset = (tt * nv + sv) * vd
    lanes = stat_all.shape[-1]

    def hits(q):
        columns = offset + q * cw + lax.broadcasted_iota(jnp.int32, (tokens, cw), 1)
        return (columns == targets[...]).astype(jnp.float32)

    def over(function, join):
        return functools.reduce(join, [function(q) for q in range(nq)])

    def add(a, b):
        return a + b

    def total(values):
        return jnp.sum(values, axis=1, keepdims=True)

    top_t = over(lambda q: jnp.max(logits_t[q], axis=1, keepdims=True), jnp.maximum)
    top_s = over(lambda q: jnp.max(logits_s[q], axis=1, keepdims=True), jnp.maximum)
    sums = [jnp.zeros((tokens, 1), jnp.float32) for _ in range(5)]
    for q in range(nq):
        lt, ls = logits_t[q] - top_t, logits_s[q]
        et = jnp.exp(lt)
        here = (et, et * ls, et * lt, jnp.exp(ls - top_s), hits(q) * ls)
        sums = [old + total(new) for old, new in zip(sums, here)]
    eye = lax.broadcasted_iota(jnp.int32, (tokens, lanes), 0) == lax.broadcasted_iota(jnp.int32, (tokens, lanes), 1)

    def to_row(column):
        return jnp.sum(jnp.where(eye, column, 0.0), axis=0, keepdims=True)

    def to_column(row):
        return jnp.sum(jnp.where(eye, row, 0.0), axis=1, keepdims=True)

    stats = [top_t, sums[0], sums[1], sums[2], top_s, sums[3], sums[4]]
    stat_all[core, tt, z] = jnp.concatenate(
        [to_row(x) for x in stats] + [jnp.zeros((1, lanes), jnp.float32)], axis=0
    )
    stat_gather = (stat_all, stat_send, stat_recv)
    start_all(gather_z(*stat_gather))
    gather_z_wait(*stat_gather)
    start_all(gather_tt(*stat_gather))
    gather_tt_wait(*stat_gather)
    gather_core(*stat_gather).start()
    gather_core_wait(*stat_gather)

    every = stat_all[...].reshape((2 * ntt * nz, 8, lanes))
    peak = jnp.max(every, axis=0)
    scale = jnp.exp(every - peak[None])
    wt, ws = scale[:, 0, :], scale[:, 4, :]
    real = lax.broadcasted_iota(jnp.int32, (1, lanes), 1) < tokens

    def joined(values):
        return jnp.where(real, jnp.sum(values, axis=0, keepdims=True), 1.0)

    sum_t = joined(wt * every[:, 1, :])
    sum_s = joined(ws * every[:, 5, :])
    log_t = jnp.log(sum_t)
    mass = joined(wt * every[:, 1, :]) / sum_t
    cross = joined(wt * every[:, 2, :]) / sum_t
    shifted = every[:, 3, :] + (every[:, 0, :] - peak[0:1]) * every[:, 1, :]
    entropy = joined(wt * shifted) / sum_t - mass * log_t
    norm_s = peak[4:5] + jnp.log(sum_s)
    picked = joined(every[:, 6, :])
    per_row = entropy - (cross - mass * norm_s) + ce_weight * (norm_s - picked)
    loss_ref[0, 0] = jnp.sum(jnp.where(real, per_row, 0.0)) / tokens

    norm_t_col = to_column(peak[0:1] + log_t)
    norm_s_col = to_column(norm_s)
    mass_col = to_column(mass)
    for q in range(nq):
        probs = jnp.exp(logits_t[q] - norm_t_col).astype(jnp.bfloat16).astype(jnp.float32)
        grad = (mass_col + ce_weight) * jnp.exp(logits_s[q] - norm_s_col) - probs - ce_weight * hits(q)
        grad_ref[:, q * cw : (q + 1) * cw] = grad.astype(jnp.bfloat16)

    half = ds // 2
    width = 512
    for who, target in ((1 - core, hg_out), (core, hg_own)):

        @pl.loop(0, half // width)
        def _(n):
            start = pl.multiple_of(who * half + n * width, 128)
            target[:, pl.ds(pl.multiple_of(n * width, 128), width)] = lax.dot_general(
                grad_ref[...], w_buf[pl.ds(start, width), :], (((1,), (1,)), ((), ())),
                preferred_element_type=jnp.float32,
            )

        if target is hg_out:
            push(hg_out, hg_in, hg_send.at[0], hg_recv.at[0], sibling).start()
    hg_pair = push(hg_out, hg_in, hg_send.at[0], hg_recv.at[0], sibling)
    hg_pair.wait_recv()
    group = tokens // ntt
    for a in range(ntt):
        part = slice(a * group, (a + 1) * group)
        tt_out[a] = hg_own[part, :] + hg_in[part, :]
    copies = [
        push(tt_out.at[other_tt(k)], tt_in.at[tt], tt_send.at[k], tt_recv.at[tt], {"tt": other_tt(k)})
        for k in range(1, ntt)
    ]
    start_all(copies)
    here = tt_out[tt]
    for k in range(1, ntt):
        p = other_tt(k)
        push(tt_in.at[p], tt_in.at[p], tt_send.at[k], tt_recv.at[p], {"tt": p}).wait_recv()
        here = here + tt_in[p]
    for b in range(nz):
        z_out[b] = here[b * 2 * rows : (b + 1) * 2 * rows, :]
    z_copies = [
        push(z_out.at[other_z(k)], z_in.at[z], z_send.at[k], z_recv.at[z], {"sv": other_z(k) * 2 + core})
        for k in range(1, nz)
    ]
    start_all(z_copies)
    here = z_out[z]
    for k in range(1, nz):
        p = other_z(k)
        push(z_in.at[p], z_in.at[p], z_send.at[k], z_recv.at[p], {"sv": p * 2 + core}).wait_recv()
        here = here + z_in[p]
    for c in range(2):
        c_out[c] = here[c * rows : (c + 1) * rows, :]
    last = push(c_out.at[1 - core], c_in, hg_send.at[1], hg_recv.at[1], sibling)
    last.start()
    hgrad_ref[:, pl.ds(pl.multiple_of(core * half, 128), half)] = c_out[core]
    last.wait_recv()
    hgrad_ref[:, pl.ds(pl.multiple_of((1 - core) * half, 128), half)] = c_in[...]

    last.wait_send()
    hg_pair.wait_send()
    for copy in copies + z_copies:
        copy.wait_send()
    gather_sent(*hid_gather)
    gather_sent(*stat_gather)

    @pl.loop(0, steps)
    def _(s):
        sib_copy(s).wait_send()

        @pl.when(s < outer)
        def _():
            line_copy(s).wait_send()


def head_kernel(hid_ref, grad_ref, out_ref):
    out_ref[...] = lax.dot_general(
        hid_ref[...], grad_ref[...], (((0,), (0,)), ((), ())), preferred_element_type=jnp.float32
    ).astype(out_ref.dtype)


def body(ntt, nv, teacher_hidden, teacher_head, student_hidden, student_head, targets):
    f32, bf16 = jnp.float32, jnp.bfloat16
    tokens, dt = teacher_hidden.shape
    rows = student_hidden.shape[0]
    ds, vd = student_head.shape
    nz = nv // 2
    cw = min(vd, 512)
    nq = vd // cw
    steps = nz * nq
    lanes = -(-tokens // 128) * 128
    half = ds // 2
    sems = pltpu.SemaphoreType.DMA
    vmem = pl.BlockSpec(memory_space=pltpu.VMEM)
    hbm = pl.BlockSpec(memory_space=pl.ANY)
    shards = (nz, nq, tokens, cw)
    peers = nz + ntt + 1
    loss, hid, grad, hidden_grad = pl.pallas_call(
        functools.partial(kernel, ntt, nv, nq),
        out_shape=(
            jax.ShapeDtypeStruct((1, 1), f32),
            jax.ShapeDtypeStruct((tokens, ds), bf16),
            jax.ShapeDtypeStruct((tokens, vd), bf16),
            jax.ShapeDtypeStruct((rows, ds), f32),
        ),
        in_specs=[vmem, hbm, vmem, hbm, vmem],
        out_specs=(pl.BlockSpec(memory_space=pltpu.SMEM), vmem, vmem, vmem),
        scratch_shapes=[
            pltpu.VMEM((depth, dt, cw), bf16),
            pltpu.VMEM((ds, vd), bf16),
            pltpu.VMEM(shards, f32),
            pltpu.VMEM(shards, f32),
            pltpu.VMEM(shards, f32),
            pltpu.VMEM((2,) + shards, f32),
            pltpu.VMEM(shards[1:], f32),
            pltpu.VMEM(shards[1:], f32),
            pltpu.VMEM((2, ntt, nz, rows, ds), f32),
            pltpu.VMEM((tokens, ds), f32),
            pltpu.VMEM((2, ntt, nz, 8, lanes), f32),
            pltpu.VMEM((tokens, half), f32),
            pltpu.VMEM((tokens, half), f32),
            pltpu.VMEM((tokens, half), f32),
            pltpu.VMEM((ntt, tokens // ntt, half), f32),
            pltpu.VMEM((ntt, tokens // ntt, half), f32),
            pltpu.VMEM((nz, 2 * rows, half), f32),
            pltpu.VMEM((nz, 2 * rows, half), f32),
            pltpu.VMEM((2, rows, half), f32),
            pltpu.VMEM((rows, half), f32),
            sems((depth,)),
            sems,
            sems((steps,)),
            sems((steps,)),
            sems((steps,)),
            sems((2, nz, nq)),
            sems((peers,)),
            sems((peers,)),
            sems((peers,)),
            sems((peers,)),
            sems((2,)),
            sems((2,)),
            sems((ntt,)),
            sems((ntt,)),
            sems((nz,)),
            sems((nz,)),
        ],
        compiler_params=pltpu.CompilerParams(
            collective_id=0, has_side_effects=True, vmem_limit_bytes=60 * 2**20
        ),
    )(teacher_hidden, teacher_head, student_hidden, student_head, targets.reshape(tokens, 1))
    block = 512
    head_grad = pl.pallas_call(
        head_kernel,
        grid=(ds // block,),
        out_shape=jax.ShapeDtypeStruct((ds, vd), bf16),
        in_specs=[
            pl.BlockSpec((tokens, block), lambda i: (0, i)),
            pl.BlockSpec((tokens, vd), lambda i: (0, 0)),
        ],
        out_specs=pl.BlockSpec((block, vd), lambda i: (i, 0)),
        compiler_params=pltpu.CompilerParams(vmem_limit_bytes=32 * 2**20),
    )(hid, grad)
    return (loss.reshape(()), head_grad, hidden_grad)


def solution(mesh):
    placed = (P(None, "sv"), P("sv", "tt"), P(("tt", "sv"), None), P(None, ("tt", "sv")), P())
    return jax.shard_map(
        functools.partial(body, mesh.shape["tt"], mesh.shape["sv"]),
        mesh=mesh,
        in_specs=placed,
        out_specs=(P(), P(None, ("tt", "sv")), P(("tt", "sv"), None)),
        check_vma=False,
    )
```

```python
import functools

import jax
import jax.numpy as jnp
from jax import lax
from jax.experimental import pallas as pl
from jax.experimental.pallas import tpu as pltpu
from jax.sharding import PartitionSpec as P

MESH = pl.DeviceIdType.MESH
ce_weight = 0.5
depth = 6
lag = 5


def visit_order(nz):
    table = []
    for z in range(nz):
        right, left = list(range(nz - 1, z, -1)), list(range(z))
        first, second = (right, left) if len(right) >= len(left) else (left, right)
        order = []
        while first or second:
            if first:
                order.append(first.pop(0))
            if second:
                order.append(second.pop(0))
        table.append(order + [z])
    return table


def lookup(table, row, column):
    value = jnp.int32(0)
    for r, entries in enumerate(table):
        for c, entry in enumerate(entries):
            if entry:
                value = jnp.where((row == r) & (column == c), jnp.int32(entry), value)
    return value


def kernel(
    ntt, nv, nq,
    t_hidden, t_head, s_hidden, s_head, targets,
    loss_ref, hid_t_ref, grad_ref, hgrad_ref,
    t_buf, w_buf, mine, sib_out, sib_in, line_in, logits_t, logits_s,
    hid_all, hid_f, hid_ref, stat_all, hg_out, hg_in, hg_own, tt_out, tt_in, z_out, z_in, c_out, c_in,
    t_sem, w_sem, sib_send, sib_recv, line_send, line_recv,
    hid_send, hid_recv, stat_send, stat_recv, hg_send, hg_recv, tt_send, tt_recv, z_send, z_recv,
):
    nz = nv // 2
    tt, sv = lax.axis_index("tt"), lax.axis_index("sv")
    z, core = sv // 2, sv % 2
    tokens = t_hidden.shape[0]
    vd = s_head.shape[1]
    ds = s_head.shape[0]
    cw = vd // nq
    steps = nz * nq
    table = visit_order(nz)

    def other_z(k):
        return lax.rem(z + k, nz)

    def other_tt(k):
        return lax.rem(tt + k, ntt)

    here_at = core * ntt + tt

    def beside(k):
        at = lax.rem(here_at + k, 2 * ntt)
        return at, {"tt": lax.rem(at, ntt), "sv": z * 2 + at // ntt}

    def push(src, dst, send, recv, where):
        return pltpu.make_async_remote_copy(
            src_ref=src, dst_ref=dst, send_sem=send, recv_sem=recv, device_id=where, device_id_type=MESH
        )

    sibling = {"sv": z * 2 + (1 - core)}

    def piece(i):
        s, half = i // 2, i % 2
        dest = lookup(table, z, s // nq)
        who = jnp.where(half == 0, 1 - core, core)
        start = pl.multiple_of((dest * 2 + who) * vd + (s % nq) * cw, 128)
        slot = lax.rem(i, depth)
        return pltpu.make_async_copy(t_head.at[:, pl.ds(start, cw)], t_buf.at[slot], t_sem.at[slot])

    for i in range(min(depth, 2 * steps)):
        piece(jnp.int32(i)).start()
    student = pltpu.make_async_copy(s_head, w_buf, w_sem)

    barrier = pltpu.get_barrier_semaphore()
    for k in range(1, nz):
        pl.semaphore_signal(barrier, inc=1, device_id={"sv": other_z(k) * 2 + core}, device_id_type=MESH)
    for k in range(1, 2 * ntt):
        pl.semaphore_signal(barrier, inc=1, device_id=beside(k)[1], device_id_type=MESH)
    pl.semaphore_wait(barrier, nz + 2 * ntt - 2)

    def gather_z(buf, send, recv):
        return [
            push(
                buf.at[here_at, z], buf.at[here_at, z], send.at[k], recv.at[z], {"sv": other_z(k) * 2 + core}
            )
            for k in range(1, nz)
        ]

    def gather_z_wait(buf, send, recv):
        for k in range(1, nz):
            p = other_z(k)
            ref = buf.at[here_at, p]
            push(ref, ref, send.at[k], recv.at[p], {"sv": p * 2 + core}).wait_recv()

    def gather_rest(buf, send, recv):
        return [
            push(buf.at[here_at], buf.at[here_at], send.at[nz + k], recv.at[nz + here_at], beside(k)[1])
            for k in range(1, 2 * ntt)
        ]

    def gather_rest_wait(buf, send, recv):
        for k in range(1, 2 * ntt):
            at, where = beside(k)
            push(buf.at[at], buf.at[at], send.at[nz + k], recv.at[nz + at], where).wait_recv()

    def start_all(copies):
        for copy in copies:
            copy.start()

    def gather_sent(buf, send, recv):
        for copy in gather_z(buf, send, recv) + gather_rest(buf, send, recv):
            copy.wait_send()

    hid_gather = (hid_all, hid_send, hid_recv)
    hid_all[here_at, z] = s_hidden[...].astype(jnp.float32)
    start_all(gather_z(*hid_gather))

    def sib_copy(s):
        dest, q = lookup(table, z, s // nq), s % nq
        return push(sib_out.at[dest, q], sib_in.at[dest, q], sib_send.at[s], sib_recv.at[s], sibling)

    def line_copy(s):
        dest, q = lookup(table, z, s // nq), s % nq
        side = jnp.where(dest > z, 0, 1)
        onto = jnp.where(dest > z, z + 1, z - 1)
        return push(
            mine.at[dest, q], line_in.at[side, dest, q], line_send.at[s], line_recv.at[side, dest, q],
            {"sv": onto * 2 + core},
        )

    def line_arrived(side, dest, q):
        ref = line_in.at[side, dest, q]
        push(ref, ref, line_send.at[0], line_recv.at[side, dest, q], sibling).wait_recv()

    def pair(s):
        sib_copy(s).wait_recv()
        dest, q = lookup(table, z, s // nq), s % nq
        mine[dest, q] += sib_in[dest, q]

    def forward(s):
        dest, q = lookup(table, z, s // nq), s % nq
        side = jnp.where(dest > z, 0, 1)
        upstream = jnp.where(dest > z, z > 0, z < nz - 1)

        @pl.when(upstream)
        def _():
            line_arrived(side, dest, q)
            mine[dest, q] += line_in[side, dest, q]

        line_copy(s).start()

    outer = (nz - 1) * nq
    at_end = (z == 0) | (z == nz - 1)

    @pl.loop(0, steps)
    def _(s):
        dest, q = lookup(table, z, s // nq), s % nq
        for half, target in ((0, sib_out), (1, mine)):
            i = 2 * s + half
            piece(i).wait()
            target[dest, q] = jnp.dot(
                t_hidden[...], t_buf[lax.rem(i, depth)], preferred_element_type=jnp.float32
            )
            if half == 0:
                sib_copy(s).start()

            @pl.when(i + depth < 2 * steps)
            def _():
                piece(i + depth).start()

        @pl.when(s == max(0, steps - 4))
        def _():
            student.start()

        @pl.when(s >= 1)
        def _():
            pair(s - 1)

        late = jnp.where(at_end, s - 1, s - lag)

        @pl.when((late >= 0) & (late < outer))
        def _():
            forward(late)

        @pl.when(s == steps // 4)
        def _():
            gather_z_wait(*hid_gather)
            start_all(gather_rest(*hid_gather))

    pair(jnp.int32(steps - 1))

    @pl.when(at_end)
    def _():
        for late in range(steps - 1, outer):
            forward(jnp.int32(late))

    left = list(range(max(0, steps - lag), outer))

    def forward_next():
        if left:
            late = left.pop(0)

            @pl.when(jnp.logical_not(at_end))
            def _():
                forward(jnp.int32(late))

    while len(left) > nq:
        forward_next()

    gather_rest_wait(*hid_gather)
    rows = s_hidden.shape[0]
    for a in range(ntt):
        for b in range(nz):
            for c in range(2):
                at = (a * nv + b * 2 + c) * rows
                hid_f[at : at + rows, :] = hid_all[c * ntt + a, b]
    hid_ref[...] = hid_f[...].astype(jnp.bfloat16)

    student.wait()

    for n in range(nq):
        logits_s[n] = jnp.dot(
            hid_ref[...], w_buf[:, n * cw : (n + 1) * cw], preferred_element_type=jnp.float32
        )
        forward_next()

    for q in range(nq):
        logits_t[q] = mine[z, q]
        for side, there in ((0, z > 0), (1, z < nz - 1)):

            @pl.when(there)
            def _():
                line_arrived(side, z, q)
                logits_t[q] += line_in[side, z, q]

    offset = (tt * nv + sv) * vd
    lanes = stat_all.shape[-1]

    square = lax.broadcasted_iota(jnp.int32, (tokens, tokens), 0) == lax.broadcasted_iota(
        jnp.int32, (tokens, tokens), 1
    )
    wanted = jnp.sum(jnp.where(square, targets[...], 0), axis=1, keepdims=True)

    def hits(q):
        columns = offset + q * cw + lax.broadcasted_iota(jnp.int32, (tokens, cw), 1)
        return (columns == wanted).astype(jnp.float32)

    def over(function, join):
        return functools.reduce(join, [function(q) for q in range(nq)])

    def add(a, b):
        return a + b

    def total(values):
        return jnp.sum(values, axis=1, keepdims=True)

    top_t = over(lambda q: jnp.max(logits_t[q], axis=1, keepdims=True), jnp.maximum)
    top_s = over(lambda q: jnp.max(logits_s[q], axis=1, keepdims=True), jnp.maximum)
    sums = [jnp.zeros((tokens, 1), jnp.float32) for _ in range(5)]
    for q in range(nq):
        lt, ls = logits_t[q] - top_t, logits_s[q]
        et = jnp.exp(lt)
        here = (et, et * ls, et * lt, jnp.exp(ls - top_s), hits(q) * ls)
        sums = [old + total(new) for old, new in zip(sums, here)]
        logits_t[q], logits_s[q] = et, here[3]
    eye = lax.broadcasted_iota(jnp.int32, (tokens, lanes), 0) == lax.broadcasted_iota(jnp.int32, (tokens, lanes), 1)

    def to_row(column):
        return jnp.sum(jnp.where(eye, column, 0.0), axis=0, keepdims=True)

    def to_column(row):
        return jnp.sum(jnp.where(eye, row, 0.0), axis=1, keepdims=True)

    stats = [top_t, sums[0], sums[1], sums[2], top_s, sums[3], sums[4]]
    stat_all[here_at, z] = jnp.concatenate(
        [to_row(x) for x in stats] + [jnp.zeros((1, lanes), jnp.float32)], axis=0
    )
    stat_gather = (stat_all, stat_send, stat_recv)
    start_all(gather_z(*stat_gather))
    hid_t_ref[...] = hid_f[...].T.astype(jnp.bfloat16)
    gather_z_wait(*stat_gather)
    start_all(gather_rest(*stat_gather))
    gather_rest_wait(*stat_gather)

    every = stat_all[...].reshape((2 * ntt * nz, 8, lanes))
    peak = jnp.max(every, axis=0)
    scale = jnp.exp(every - peak[None])
    wt, ws = scale[:, 0, :], scale[:, 4, :]
    real = lax.broadcasted_iota(jnp.int32, (1, lanes), 1) < tokens

    def joined(values):
        return jnp.where(real, jnp.sum(values, axis=0, keepdims=True), 1.0)

    sum_t = joined(wt * every[:, 1, :])
    sum_s = joined(ws * every[:, 5, :])
    log_t = jnp.log(sum_t)
    mass = joined(wt * every[:, 1, :]) / sum_t
    cross = joined(wt * every[:, 2, :]) / sum_t
    shifted = every[:, 3, :] + (every[:, 0, :] - peak[0:1]) * every[:, 1, :]
    entropy = joined(wt * shifted) / sum_t - mass * log_t
    norm_s = peak[4:5] + jnp.log(sum_s)
    picked = joined(every[:, 6, :])
    per_row = entropy - (cross - mass * norm_s) + ce_weight * (norm_s - picked)
    loss_ref[0, 0] = jnp.sum(jnp.where(real, per_row, 0.0)) / tokens

    scale_t = jnp.exp(top_t - to_column(peak[0:1] + log_t))
    scale_s = (to_column(mass) + ce_weight) * jnp.exp(top_s - to_column(norm_s))
    for q in range(nq):
        probs = (logits_t[q] * scale_t).astype(jnp.bfloat16).astype(jnp.float32)
        grad = scale_s * logits_s[q] - probs - ce_weight * hits(q)
        grad_ref[:, q * cw : (q + 1) * cw] = grad.astype(jnp.bfloat16)

    half = ds // 2
    pieces, width = hg_out.shape[0], hg_out.shape[2]
    group = tokens // ntt

    def product(who, p):
        start = pl.multiple_of(who * half + p * width, 128)
        return lax.dot_general(
            grad_ref[...], w_buf[pl.ds(start, width), :], (((1,), (1,)), ((), ())),
            preferred_element_type=jnp.float32,
        )

    def core_copy(p):
        return push(hg_out.at[p], hg_in.at[p], hg_send.at[p], hg_recv.at[p], sibling)

    def tt_copies(p):
        return [
            push(
                tt_out.at[p, other_tt(k)], tt_in.at[p, tt], tt_send.at[p, k], tt_recv.at[p, tt],
                {"tt": other_tt(k)},
            )
            for k in range(1, ntt)
        ]

    def z_copies(p):
        return [
            push(
                z_out.at[p, other_z(k)], z_in.at[p, z], z_send.at[p, k], z_recv.at[p, z],
                {"sv": other_z(k) * 2 + core},
            )
            for k in range(1, nz)
        ]

    def to_tt(p):
        core_copy(p).wait_recv()
        for a in range(ntt):
            part = slice(a * group, (a + 1) * group)
            tt_out[p, a] = hg_own[p, part, :] + hg_in[p, part, :]
        start_all(tt_copies(p))

    def to_z(p):
        here = tt_out[p, tt]
        for k in range(1, ntt):
            o = other_tt(k)
            ref = tt_in.at[p, o]
            push(ref, ref, tt_send.at[p, k], tt_recv.at[p, o], {"tt": o}).wait_recv()
            here = here + tt_in[p, o]
        for b in range(nz):
            z_out[p, b] = here[b * 2 * rows : (b + 1) * 2 * rows, :]
        start_all(z_copies(p))

    for p in range(pieces + 2):
        if p < pieces:
            hg_out[p] = product(1 - core, p)
            core_copy(p).start()
            hg_own[p] = product(core, p)
        if 1 <= p <= pieces:
            to_tt(p - 1)
        if p >= 2:
            to_z(p - 2)
    for p in range(pieces):
        here = z_out[p, z]
        for k in range(1, nz):
            o = other_z(k)
            ref = z_in.at[p, o]
            push(ref, ref, z_send.at[p, k], z_recv.at[p, o], {"sv": o * 2 + core}).wait_recv()
            here = here + z_in[p, o]
        for c in range(2):
            c_out[c, :, p * width : (p + 1) * width] = here[c * rows : (c + 1) * rows, :]
    last = push(c_out.at[1 - core], c_in, hg_send.at[pieces], hg_recv.at[pieces], sibling)
    last.start()
    hgrad_ref[:, pl.ds(pl.multiple_of(core * half, 128), half)] = c_out[core]
    last.wait_recv()
    hgrad_ref[:, pl.ds(pl.multiple_of((1 - core) * half, 128), half)] = c_in[...]

    last.wait_send()
    for p in range(pieces):
        for copy in [core_copy(p)] + tt_copies(p) + z_copies(p):
            copy.wait_send()
    gather_sent(*hid_gather)
    gather_sent(*stat_gather)

    @pl.loop(0, steps)
    def _(s):
        sib_copy(s).wait_send()

        @pl.when(s < outer)
        def _():
            line_copy(s).wait_send()


def head_kernel(hid_t_ref, grad_ref, out_ref):
    out_ref[...] = lax.dot_general(
        hid_t_ref[...], grad_ref[...], (((1,), (0,)), ((), ())), preferred_element_type=jnp.float32
    ).astype(out_ref.dtype)


def body(ntt, nv, teacher_hidden, teacher_head, student_hidden, student_head, targets):
    f32, bf16 = jnp.float32, jnp.bfloat16
    tokens, dt = teacher_hidden.shape
    rows = student_hidden.shape[0]
    ds, vd = student_head.shape
    nz = nv // 2
    cw = min(vd, 512)
    nq = vd // cw
    steps = nz * nq
    lanes = -(-tokens // 128) * 128
    half = ds // 2
    sems = pltpu.SemaphoreType.DMA
    vmem = pl.BlockSpec(memory_space=pltpu.VMEM)
    hbm = pl.BlockSpec(memory_space=pl.ANY)
    shards = (nz, nq, tokens, cw)
    peers = nz + 2 * ntt
    width = min(half, 512)
    pieces = half // width
    loss, hid_t, grad, hidden_grad = pl.pallas_call(
        functools.partial(kernel, ntt, nv, nq),
        out_shape=(
            jax.ShapeDtypeStruct((1, 1), f32),
            jax.ShapeDtypeStruct((ds, tokens), bf16),
            jax.ShapeDtypeStruct((tokens, vd), bf16),
            jax.ShapeDtypeStruct((rows, ds), f32),
        ),
        in_specs=[vmem, hbm, vmem, hbm, vmem],
        out_specs=(pl.BlockSpec(memory_space=pltpu.SMEM), vmem, vmem, vmem),
        scratch_shapes=[
            pltpu.VMEM((depth, dt, cw), bf16),
            pltpu.VMEM((ds, vd), bf16),
            pltpu.VMEM(shards, f32),
            pltpu.VMEM(shards, f32),
            pltpu.VMEM(shards, f32),
            pltpu.VMEM((2,) + shards, f32),
            pltpu.VMEM(shards[1:], f32),
            pltpu.VMEM(shards[1:], f32),
            pltpu.VMEM((2 * ntt, nz, rows, ds), f32),
            pltpu.VMEM((tokens, ds), f32),
            pltpu.VMEM((tokens, ds), bf16),
            pltpu.VMEM((2 * ntt, nz, 8, lanes), f32),
            pltpu.VMEM((pieces, tokens, width), f32),
            pltpu.VMEM((pieces, tokens, width), f32),
            pltpu.VMEM((pieces, tokens, width), f32),
            pltpu.VMEM((pieces, ntt, tokens // ntt, width), f32),
            pltpu.VMEM((pieces, ntt, tokens // ntt, width), f32),
            pltpu.VMEM((pieces, nz, 2 * rows, width), f32),
            pltpu.VMEM((pieces, nz, 2 * rows, width), f32),
            pltpu.VMEM((2, rows, half), f32),
            pltpu.VMEM((rows, half), f32),
            sems((depth,)),
            sems,
            sems((steps,)),
            sems((steps,)),
            sems((steps,)),
            sems((2, nz, nq)),
            sems((peers,)),
            sems((peers,)),
            sems((peers,)),
            sems((peers,)),
            sems((pieces + 1,)),
            sems((pieces + 1,)),
            sems((pieces, ntt)),
            sems((pieces, ntt)),
            sems((pieces, nz)),
            sems((pieces, nz)),
        ],
        compiler_params=pltpu.CompilerParams(
            collective_id=0, has_side_effects=True, vmem_limit_bytes=60 * 2**20
        ),
    )(teacher_hidden, teacher_head, student_hidden, student_head, targets.reshape(1, tokens))
    block = 512
    head_grad = pl.pallas_call(
        head_kernel,
        grid=(ds // block,),
        out_shape=jax.ShapeDtypeStruct((ds, vd), bf16),
        in_specs=[
            pl.BlockSpec((block, tokens), lambda i: (i, 0)),
            pl.BlockSpec((tokens, vd), lambda i: (0, 0)),
        ],
        out_specs=pl.BlockSpec((block, vd), lambda i: (i, 0)),
        compiler_params=pltpu.CompilerParams(vmem_limit_bytes=60 * 2**20),
    )(hid_t, grad)
    return (loss.reshape(()), head_grad, hidden_grad)


def solution(mesh):
    placed = (P(None, "sv"), P("sv", "tt"), P(("tt", "sv"), None), P(None, ("tt", "sv")), P())
    return jax.shard_map(
        functools.partial(body, mesh.shape["tt"], mesh.shape["sv"]),
        mesh=mesh,
        in_specs=placed,
        out_specs=(P(), P(None, ("tt", "sv")), P(("tt", "sv"), None)),
        check_vma=False,
    )
```

```python
import functools

import jax
import jax.numpy as jnp
from jax import lax
from jax.experimental import pallas as pl
from jax.experimental.pallas import tpu as pltpu
from jax.sharding import PartitionSpec as P

MESH = pl.DeviceIdType.MESH
ce_weight = 0.5
depth = 6
lag = 5


def visit_order(nz):
    table = []
    for z in range(nz):
        right, left = list(range(nz - 1, z, -1)), list(range(z))
        first, second = (right, left) if len(right) >= len(left) else (left, right)
        order = []
        while first or second:
            if first:
                order.append(first.pop(0))
            if second:
                order.append(second.pop(0))
        table.append(order + [z])
    return table


def lookup(table, row, column):
    value = jnp.int32(0)
    for r, entries in enumerate(table):
        for c, entry in enumerate(entries):
            if entry:
                value = jnp.where((row == r) & (column == c), jnp.int32(entry), value)
    return value


def kernel(
    ntt, nv, nq,
    t_hidden, t_head, s_hidden, s_head, targets,
    loss_ref, hid_t_ref, grad_ref, hgrad_ref,
    t_buf, w_buf, mine, sib_out, sib_in, line_in, logits_t, logits_s,
    hid_all, hid_f, hid_ref, grad_t, stat_all, hg_out, hg_in, hg_own, tt_out, tt_in, z_out, z_in, c_out, c_in,
    t_sem, w_sem, sib_send, sib_recv, line_send, line_recv,
    hid_send, hid_recv, stat_send, stat_recv, hg_send, hg_recv, tt_send, tt_recv, z_send, z_recv,
):
    nz = nv // 2
    tt, sv = lax.axis_index("tt"), lax.axis_index("sv")
    z, core = sv // 2, sv % 2
    tokens = t_hidden.shape[0]
    vd = s_head.shape[1]
    ds = s_head.shape[0]
    cw = vd // nq
    steps = nz * nq
    table = visit_order(nz)

    def other_z(k):
        return lax.rem(z + k, nz)

    def other_tt(k):
        return lax.rem(tt + k, ntt)

    here_at = core * ntt + tt

    def beside(k):
        at = lax.rem(here_at + k, 2 * ntt)
        return at, {"tt": lax.rem(at, ntt), "sv": z * 2 + at // ntt}

    def push(src, dst, send, recv, where):
        return pltpu.make_async_remote_copy(
            src_ref=src, dst_ref=dst, send_sem=send, recv_sem=recv, device_id=where, device_id_type=MESH
        )

    sibling = {"sv": z * 2 + (1 - core)}

    def piece(i):
        s, half = i // 2, i % 2
        dest = lookup(table, z, s // nq)
        who = jnp.where(half == 0, 1 - core, core)
        start = pl.multiple_of((dest * 2 + who) * vd + (s % nq) * cw, 128)
        slot = lax.rem(i, depth)
        return pltpu.make_async_copy(t_head.at[:, pl.ds(start, cw)], t_buf.at[slot], t_sem.at[slot])

    for i in range(min(depth, 2 * steps)):
        piece(jnp.int32(i)).start()
    student = pltpu.make_async_copy(s_head, w_buf, w_sem)

    barrier = pltpu.get_barrier_semaphore()
    for k in range(1, nz):
        pl.semaphore_signal(barrier, inc=1, device_id={"sv": other_z(k) * 2 + core}, device_id_type=MESH)
    for k in range(1, 2 * ntt):
        pl.semaphore_signal(barrier, inc=1, device_id=beside(k)[1], device_id_type=MESH)
    pl.semaphore_wait(barrier, nz + 2 * ntt - 2)

    def gather_z(buf, send, recv):
        return [
            push(
                buf.at[here_at, z], buf.at[here_at, z], send.at[k], recv.at[z], {"sv": other_z(k) * 2 + core}
            )
            for k in range(1, nz)
        ]

    def gather_z_wait(buf, send, recv):
        for k in range(1, nz):
            p = other_z(k)
            ref = buf.at[here_at, p]
            push(ref, ref, send.at[k], recv.at[p], {"sv": p * 2 + core}).wait_recv()

    def gather_rest(buf, send, recv):
        return [
            push(buf.at[here_at], buf.at[here_at], send.at[nz + k], recv.at[nz + here_at], beside(k)[1])
            for k in range(1, 2 * ntt)
        ]

    def gather_rest_wait(buf, send, recv):
        for k in range(1, 2 * ntt):
            at, where = beside(k)
            push(buf.at[at], buf.at[at], send.at[nz + k], recv.at[nz + at], where).wait_recv()

    def start_all(copies):
        for copy in copies:
            copy.start()

    def gather_sent(buf, send, recv):
        for copy in gather_z(buf, send, recv) + gather_rest(buf, send, recv):
            copy.wait_send()

    hid_gather = (hid_all, hid_send, hid_recv)
    hid_all[here_at, z] = s_hidden[...].astype(jnp.float32)
    start_all(gather_z(*hid_gather))

    def sib_copy(s):
        dest, q = lookup(table, z, s // nq), s % nq
        return push(sib_out.at[dest, q], sib_in.at[dest, q], sib_send.at[s], sib_recv.at[s], sibling)

    def line_copy(s):
        dest, q = lookup(table, z, s // nq), s % nq
        side = jnp.where(dest > z, 0, 1)
        onto = jnp.where(dest > z, z + 1, z - 1)
        return push(
            mine.at[dest, q], line_in.at[side, dest, q], line_send.at[s], line_recv.at[side, dest, q],
            {"sv": onto * 2 + core},
        )

    def line_arrived(side, dest, q):
        ref = line_in.at[side, dest, q]
        push(ref, ref, line_send.at[0], line_recv.at[side, dest, q], sibling).wait_recv()

    def pair(s):
        sib_copy(s).wait_recv()
        dest, q = lookup(table, z, s // nq), s % nq
        mine[dest, q] += sib_in[dest, q]

    def forward(s):
        dest, q = lookup(table, z, s // nq), s % nq
        side = jnp.where(dest > z, 0, 1)
        upstream = jnp.where(dest > z, z > 0, z < nz - 1)

        @pl.when(upstream)
        def _():
            line_arrived(side, dest, q)
            mine[dest, q] += line_in[side, dest, q]

        line_copy(s).start()

    outer = (nz - 1) * nq
    at_end = (z == 0) | (z == nz - 1)

    @pl.loop(0, steps)
    def _(s):
        dest, q = lookup(table, z, s // nq), s % nq
        for half, target in ((0, sib_out), (1, mine)):
            i = 2 * s + half
            piece(i).wait()
            target[dest, q] = jnp.dot(
                t_hidden[...], t_buf[lax.rem(i, depth)], preferred_element_type=jnp.float32
            )
            if half == 0:
                sib_copy(s).start()

            @pl.when(i + depth < 2 * steps)
            def _():
                piece(i + depth).start()

        @pl.when(s == max(0, steps - 4))
        def _():
            student.start()

        @pl.when(s >= 1)
        def _():
            pair(s - 1)

        late = jnp.where(at_end, s - 1, s - lag)

        @pl.when((late >= 0) & (late < outer))
        def _():
            forward(late)

        @pl.when(s == steps // 4)
        def _():
            gather_z_wait(*hid_gather)
            start_all(gather_rest(*hid_gather))

    pair(jnp.int32(steps - 1))

    @pl.when(at_end)
    def _():
        for late in range(steps - 1, outer):
            forward(jnp.int32(late))

    left = list(range(max(0, steps - lag), outer))

    def forward_next():
        if left:
            late = left.pop(0)

            @pl.when(jnp.logical_not(at_end))
            def _():
                forward(jnp.int32(late))

    while len(left) > nq:
        forward_next()

    gather_rest_wait(*hid_gather)
    rows = s_hidden.shape[0]
    for a in range(ntt):
        for b in range(nz):
            for c in range(2):
                at = (a * nv + b * 2 + c) * rows
                hid_f[at : at + rows, :] = hid_all[c * ntt + a, b]
    hid_ref[...] = hid_f[...].astype(jnp.bfloat16)

    student.wait()

    for n in range(nq):
        logits_s[n] = jnp.dot(
            hid_ref[...], w_buf[:, n * cw : (n + 1) * cw], preferred_element_type=jnp.float32
        )
        forward_next()

    for q in range(nq):
        logits_t[q] = mine[z, q]
        for side, there in ((0, z > 0), (1, z < nz - 1)):

            @pl.when(there)
            def _():
                line_arrived(side, z, q)
                logits_t[q] += line_in[side, z, q]

    offset = (tt * nv + sv) * vd
    lanes = stat_all.shape[-1]

    square = lax.broadcasted_iota(jnp.int32, (tokens, tokens), 0) == lax.broadcasted_iota(
        jnp.int32, (tokens, tokens), 1
    )
    wanted = jnp.sum(jnp.where(square, targets[...], 0), axis=1, keepdims=True)

    def hits(q):
        columns = offset + q * cw + lax.broadcasted_iota(jnp.int32, (tokens, cw), 1)
        return (columns == wanted).astype(jnp.float32)

    def over(function, join):
        return functools.reduce(join, [function(q) for q in range(nq)])

    def add(a, b):
        return a + b

    def total(values):
        return jnp.sum(values, axis=1, keepdims=True)

    top_t = over(lambda q: jnp.max(logits_t[q], axis=1, keepdims=True), jnp.maximum)
    top_s = over(lambda q: jnp.max(logits_s[q], axis=1, keepdims=True), jnp.maximum)
    sums = [jnp.zeros((tokens, 1), jnp.float32) for _ in range(5)]
    for q in range(nq):
        lt, ls = logits_t[q] - top_t, logits_s[q]
        et = jnp.exp(lt)
        here = (et, et * ls, et * lt, jnp.exp(ls - top_s), hits(q) * ls)
        sums = [old + total(new) for old, new in zip(sums, here)]
        logits_t[q], logits_s[q] = et, here[3]
    eye = lax.broadcasted_iota(jnp.int32, (tokens, lanes), 0) == lax.broadcasted_iota(jnp.int32, (tokens, lanes), 1)

    def to_row(column):
        return jnp.sum(jnp.where(eye, column, 0.0), axis=0, keepdims=True)

    def to_column(row):
        return jnp.sum(jnp.where(eye, row, 0.0), axis=1, keepdims=True)

    stats = [top_t, sums[0], sums[1], sums[2], top_s, sums[3], sums[4]]
    stat_all[here_at, z] = jnp.concatenate(
        [to_row(x) for x in stats] + [jnp.zeros((1, lanes), jnp.float32)], axis=0
    )
    stat_gather = (stat_all, stat_send, stat_recv)
    start_all(gather_z(*stat_gather))
    hid_t_ref[...] = hid_f[...].T.astype(jnp.bfloat16)
    gather_z_wait(*stat_gather)
    start_all(gather_rest(*stat_gather))
    gather_rest_wait(*stat_gather)

    every = stat_all[...].reshape((2 * ntt * nz, 8, lanes))
    peak = jnp.max(every, axis=0)
    scale = jnp.exp(every - peak[None])
    wt, ws = scale[:, 0, :], scale[:, 4, :]
    real = lax.broadcasted_iota(jnp.int32, (1, lanes), 1) < tokens

    def joined(values):
        return jnp.where(real, jnp.sum(values, axis=0, keepdims=True), 1.0)

    sum_t = joined(wt * every[:, 1, :])
    sum_s = joined(ws * every[:, 5, :])
    log_t = jnp.log(sum_t)
    mass = joined(wt * every[:, 1, :]) / sum_t
    cross = joined(wt * every[:, 2, :]) / sum_t
    shifted = every[:, 3, :] + (every[:, 0, :] - peak[0:1]) * every[:, 1, :]
    entropy = joined(wt * shifted) / sum_t - mass * log_t
    norm_s = peak[4:5] + jnp.log(sum_s)
    picked = joined(every[:, 6, :])
    per_row = entropy - (cross - mass * norm_s) + ce_weight * (norm_s - picked)
    loss_ref[0, 0] = jnp.sum(jnp.where(real, per_row, 0.0)) / tokens

    scale_t = jnp.exp(top_t - to_column(peak[0:1] + log_t))
    scale_s = (to_column(mass) + ce_weight) * jnp.exp(top_s - to_column(norm_s))
    for q in range(nq):
        probs = (logits_t[q] * scale_t).astype(jnp.bfloat16).astype(jnp.float32)
        grad = scale_s * logits_s[q] - probs - ce_weight * hits(q)
        grad_ref[:, q * cw : (q + 1) * cw] = grad.astype(jnp.bfloat16)
        grad_t[q * cw : (q + 1) * cw, :] = grad.T.astype(jnp.bfloat16)

    half = ds // 2
    pieces, width = hg_out.shape[0], hg_out.shape[2]
    group = tokens // ntt

    def product(who, p):
        start = pl.multiple_of(who * half + p * width, 128)
        return jnp.dot(w_buf[pl.ds(start, width), :], grad_t[...], preferred_element_type=jnp.float32).T

    def core_copy(p):
        return push(hg_out.at[p], hg_in.at[p], hg_send.at[p], hg_recv.at[p], sibling)

    def tt_copies(p):
        return [
            push(
                tt_out.at[p, other_tt(k)], tt_in.at[p, tt], tt_send.at[p, k], tt_recv.at[p, tt],
                {"tt": other_tt(k)},
            )
            for k in range(1, ntt)
        ]

    def z_copies(p):
        return [
            push(
                z_out.at[p, other_z(k)], z_in.at[p, z], z_send.at[p, k], z_recv.at[p, z],
                {"sv": other_z(k) * 2 + core},
            )
            for k in range(1, nz)
        ]

    def to_tt(p):
        core_copy(p).wait_recv()
        for a in range(ntt):
            part = slice(a * group, (a + 1) * group)
            tt_out[p, a] = hg_own[p, part, :] + hg_in[p, part, :]
        start_all(tt_copies(p))

    def to_z(p):
        here = tt_out[p, tt]
        for k in range(1, ntt):
            o = other_tt(k)
            ref = tt_in.at[p, o]
            push(ref, ref, tt_send.at[p, k], tt_recv.at[p, o], {"tt": o}).wait_recv()
            here = here + tt_in[p, o]
        for b in range(nz):
            z_out[p, b] = here[b * 2 * rows : (b + 1) * 2 * rows, :]
        start_all(z_copies(p))

    for p in range(pieces + 2):
        if p < pieces:
            hg_out[p] = product(1 - core, p)
            core_copy(p).start()
            hg_own[p] = product(core, p)
        if 1 <= p <= pieces:
            to_tt(p - 1)
        if p >= 2:
            to_z(p - 2)
    for p in range(pieces):
        here = z_out[p, z]
        for k in range(1, nz):
            o = other_z(k)
            ref = z_in.at[p, o]
            push(ref, ref, z_send.at[p, k], z_recv.at[p, o], {"sv": o * 2 + core}).wait_recv()
            here = here + z_in[p, o]
        for c in range(2):
            c_out[c, :, p * width : (p + 1) * width] = here[c * rows : (c + 1) * rows, :]
    last = push(c_out.at[1 - core], c_in, hg_send.at[pieces], hg_recv.at[pieces], sibling)
    last.start()
    hgrad_ref[:, pl.ds(pl.multiple_of(core * half, 128), half)] = c_out[core]
    last.wait_recv()
    hgrad_ref[:, pl.ds(pl.multiple_of((1 - core) * half, 128), half)] = c_in[...]

    last.wait_send()
    for p in range(pieces):
        for copy in [core_copy(p)] + tt_copies(p) + z_copies(p):
            copy.wait_send()
    gather_sent(*hid_gather)
    gather_sent(*stat_gather)

    @pl.loop(0, steps)
    def _(s):
        sib_copy(s).wait_send()

        @pl.when(s < outer)
        def _():
            line_copy(s).wait_send()


def head_kernel(hid_t_ref, grad_ref, out_ref):
    tile = 256
    for n in range(out_ref.shape[1] // tile):
        part = slice(n * tile, (n + 1) * tile)
        out_ref[:, part] = jnp.dot(
            hid_t_ref[...], grad_ref[:, part], preferred_element_type=jnp.float32
        ).astype(out_ref.dtype)


def body(ntt, nv, teacher_hidden, teacher_head, student_hidden, student_head, targets):
    f32, bf16 = jnp.float32, jnp.bfloat16
    tokens, dt = teacher_hidden.shape
    rows = student_hidden.shape[0]
    ds, vd = student_head.shape
    nz = nv // 2
    cw = min(vd, 512)
    nq = vd // cw
    steps = nz * nq
    lanes = -(-tokens // 128) * 128
    half = ds // 2
    sems = pltpu.SemaphoreType.DMA
    vmem = pl.BlockSpec(memory_space=pltpu.VMEM)
    hbm = pl.BlockSpec(memory_space=pl.ANY)
    shards = (nz, nq, tokens, cw)
    peers = nz + 2 * ntt
    width = min(half, 512)
    pieces = half // width
    loss, hid_t, grad, hidden_grad = pl.pallas_call(
        functools.partial(kernel, ntt, nv, nq),
        out_shape=(
            jax.ShapeDtypeStruct((1, 1), f32),
            jax.ShapeDtypeStruct((ds, tokens), bf16),
            jax.ShapeDtypeStruct((tokens, vd), bf16),
            jax.ShapeDtypeStruct((rows, ds), f32),
        ),
        in_specs=[vmem, hbm, vmem, hbm, vmem],
        out_specs=(pl.BlockSpec(memory_space=pltpu.SMEM), vmem, vmem, vmem),
        scratch_shapes=[
            pltpu.VMEM((depth, dt, cw), bf16),
            pltpu.VMEM((ds, vd), bf16),
            pltpu.VMEM(shards, f32),
            pltpu.VMEM(shards, f32),
            pltpu.VMEM(shards, f32),
            pltpu.VMEM((2,) + shards, f32),
            pltpu.VMEM(shards[1:], f32),
            pltpu.VMEM(shards[1:], f32),
            pltpu.VMEM((2 * ntt, nz, rows, ds), f32),
            pltpu.VMEM((tokens, ds), f32),
            pltpu.VMEM((tokens, ds), bf16),
            pltpu.VMEM((vd, tokens), bf16),
            pltpu.VMEM((2 * ntt, nz, 8, lanes), f32),
            pltpu.VMEM((pieces, tokens, width), f32),
            pltpu.VMEM((pieces, tokens, width), f32),
            pltpu.VMEM((pieces, tokens, width), f32),
            pltpu.VMEM((pieces, ntt, tokens // ntt, width), f32),
            pltpu.VMEM((pieces, ntt, tokens // ntt, width), f32),
            pltpu.VMEM((pieces, nz, 2 * rows, width), f32),
            pltpu.VMEM((pieces, nz, 2 * rows, width), f32),
            pltpu.VMEM((2, rows, half), f32),
            pltpu.VMEM((rows, half), f32),
            sems((depth,)),
            sems,
            sems((steps,)),
            sems((steps,)),
            sems((steps,)),
            sems((2, nz, nq)),
            sems((peers,)),
            sems((peers,)),
            sems((peers,)),
            sems((peers,)),
            sems((pieces + 1,)),
            sems((pieces + 1,)),
            sems((pieces, ntt)),
            sems((pieces, ntt)),
            sems((pieces, nz)),
            sems((pieces, nz)),
        ],
        compiler_params=pltpu.CompilerParams(
            collective_id=0, has_side_effects=True, vmem_limit_bytes=60 * 2**20
        ),
    )(teacher_hidden, teacher_head, student_hidden, student_head, targets.reshape(1, tokens))
    block = 256
    head_grad = pl.pallas_call(
        head_kernel,
        grid=(ds // block,),
        out_shape=jax.ShapeDtypeStruct((ds, vd), bf16),
        in_specs=[
            pl.BlockSpec((block, tokens), lambda i: (i, 0)),
            pl.BlockSpec((tokens, vd), lambda i: (0, 0)),
        ],
        out_specs=pl.BlockSpec((block, vd), lambda i: (i, 0)),
        compiler_params=pltpu.CompilerParams(vmem_limit_bytes=60 * 2**20),
    )(hid_t, grad)
    return (loss.reshape(()), head_grad, hidden_grad)


def solution(mesh):
    placed = (P(None, "sv"), P("sv", "tt"), P(("tt", "sv"), None), P(None, ("tt", "sv")), P())
    return jax.shard_map(
        functools.partial(body, mesh.shape["tt"], mesh.shape["sv"]),
        mesh=mesh,
        in_specs=placed,
        out_specs=(P(), P(None, ("tt", "sv")), P(("tt", "sv"), None)),
        check_vma=False,
    )
```
